512 devices in a mesh: pair: 32 (over y_lo, z), day: 16 (over y_hi, x, core).
Axes of the slice: x: 4, y: 8 (y_hi: 2, y_lo: 4; y = y_hi * 4 + y_lo), z: 8, core: 2. Of those that a mesh axis runs over, the one named last changes fastest.
Arguments:
- spectra: bfloat16 [32, 2, 2048, 1024], P('day', None, 'pair'), may hold values from -6 to 6
- band_weights: float32 [8, 2048], replicated, may hold values from 0.05 to 1
- pair_stations: int32 [1536, 2], replicated, may hold values from 0 to 1023
- block_live: int32 [512], P(('pair', 'day')), may hold values from 1 to 3, 1152 in all
- windows: int32 [1536, 8, 2], P(('pair', 'day')), may hold values from 0 to 4096, as said below
- observed: bfloat16 [1536, 8, 4096], P(('pair', 'day')), may hold values from -6 to 6
Outputs:
- adjoint: float32 [32, 2, 2048, 1024], P('day', None, 'pair')
The draws below stay inside these ranges and needn't reach their ends.
Inputs may be any that keep to these rules, and one draw needn't show every extreme that they name: Block b holds pairs b * 3 to b * 3 + 2, and its first block_live[b] pairs are live. windows[p, k, 0] < windows[p, k, 1].
All inputs are finite; a program needn't handle non-finite values.
Results may differ from the reference program's by a relative error of at most 0.0035.
Values sent between devices are 32-bit elements; how exact they have to be, the bound alone decides.
A program may use at most 64 MiB of HBM per device.

```python
import math
import jax
import jax.numpy as jnp
import numpy as np
from jax import lax

L = 4096
BANDS = 8
STATIONS = 1024
PD = 3
NF = 2048
DAYS = 32
PAIRS = 1536
DEVICES = 512


def draw_windows(key, part):
    first_key = jax.random.fold_in(key, 11)
    second_key = jax.random.fold_in(key, 23)
    lower_lag = jax.random.randint(first_key, (PAIRS, BANDS), 0, L // 2)
    extent = jax.random.randint(second_key, (PAIRS, BANDS), L // 8, L + 1)
    upper_lag = jnp.minimum(lower_lag + extent, L)
    lower_lag = lower_lag.at[0, 0].set(0)
    upper_lag = upper_lag.at[0, 0].set(L)
    return jnp.stack([lower_lag, upper_lag], axis=-1).astype(jnp.int32)


def set_ends(array, stream_key, least, high):
    longest = array.shape.index(max(array.shape))
    spots = []
    for shift in (0, 1):
        where = [jax.random.randint(jax.random.fold_in(stream_key, axis), (), 0, length) for axis, length in enumerate(array.shape)]
        where[longest] = (where[longest] + shift) % array.shape[longest]
        spots.append(tuple(where))
    return array.at[spots[0]].set(least).at[spots[1]].set(high)


def levels(key, shape, shards, least, largest):
    gain, own = 1.0, jax.random.fold_in(key, 6)
    for position, parts in shards:
        steps = jnp.exp(jax.random.uniform(jax.random.fold_in(own, position), (parts,), jnp.float32, least / len(shards), largest / len(shards)))
        gain = gain * jnp.repeat(steps, shape[position] // parts).reshape([-1 if axis == position else 1 for axis in range(len(shape))])
    return gain


def length_profile(amount, total, reach, lean):
    weights = [(1 << 20) // math.isqrt(grade ** lean) + 1 for grade in range(2, amount + 1)]
    spare, counts = total - reach - (amount - 1), [1] * (amount - 1)
    while spare > 0:
        movable = [i for i in range(amount - 1) if counts[i] < reach]
        pool, budget = sum([weights[i] for i in movable]), spare
        for i in movable:
            more = min(reach - counts[i], max(1, budget * weights[i] // pool), spare)
            counts[i] = counts[i] + more
            spare = spare - more
    return np.array([reach] + counts)


def uneven(rng, number_of, total, most, skew):
    if number_of == 2:
        one = jax.random.randint(rng, (), max(1, total - most), min(most, total - 1) + 1)
        return jnp.stack([one, total - one])
    tallies = jnp.asarray(length_profile(number_of, total, most, skew), jnp.int32)
    couples = (number_of - 1) // 2
    giver, taker = tallies[1:1 + 2 * couples:2], tallies[2:2 + 2 * couples:2]
    margin = jnp.minimum(giver - 1, most - taker)
    shifted = jax.random.randint(jax.random.fold_in(rng, 1), (couples,), 0, 1 << 20) % (margin + 1)
    tallies = tallies.at[1:1 + 2 * couples:2].set(giver - shifted).at[2:2 + 2 * couples:2].set(taker + shifted)
    return tallies[jax.random.permutation(jax.random.fold_in(rng, 2), number_of)]


def normal_values(stream_key, shape, deviation, reach, split=(), kind=jnp.bfloat16):
    drawn = deviation * jax.random.normal(stream_key, shape, jnp.float32)
    if split:
        drawn = drawn * levels(stream_key, shape, split, -0.22, 0.18)
    return jnp.clip(drawn, -reach, reach).astype(kind)


def setup_inputs(seed: int = 0) -> dict:
    keys = jax.random.split(jax.random.key(seed), 7)
    return {
        "spectra": normal_values(keys[0], (DAYS, 2, NF, STATIONS), 1.0, 6.0, ((0, 16), (2, 32))),
        "band_weights": jnp.clip(jnp.exp(jax.random.uniform(keys[1], (BANDS, NF), jnp.float32, math.log(0.05), math.log(1.0))), 0.05, 1.0),
        "pair_stations": set_ends(jax.random.randint(keys[2], (PAIRS, 2), 0, STATIONS), jax.random.fold_in(keys[2], 1), 0, STATIONS - 1).astype(jnp.int32),
        "block_live": uneven(keys[3], DEVICES, DEVICES * PD * 3 // 4, PD, 2).astype(jnp.int32),
        "windows": draw_windows(jax.random.fold_in(keys[6], 71), 0),
        "observed": normal_values(keys[5], (PAIRS, BANDS, L), 1.0, 6.0, ((0, 512),)),
    }


def table_block(start, width, lags):
    half = lags // 2
    freqs = jnp.arange(half, dtype=jnp.int32)
    lag_index = start + jnp.arange(width, dtype=jnp.int32)
    phase = freqs[:, None] * lag_index[None, :] % lags
    angle = phase.astype(jnp.float32) * (2.0 * math.pi / lags)
    return jnp.concatenate([jnp.cos(angle), -jnp.sin(angle)], axis=0).astype(jnp.bfloat16)

def station_rows(spectra, stations):
    first_rows = jnp.take(spectra, stations[:, 0], axis=3).swapaxes(2, 3)
    second_rows = jnp.take(spectra, stations[:, 1], axis=3).swapaxes(2, 3)
    return (first_rows, second_rows)

def cross_terms(first_rows, second_rows):
    first = first_rows.astype(jnp.float32)
    second = second_rows.astype(jnp.float32)
    real_part = lax.optimization_barrier(jnp.sum(first[:, 0] * second[:, 0] + first[:, 1] * second[:, 1], axis=0))
    imag_part = lax.optimization_barrier(jnp.sum(first[:, 0] * second[:, 1] - first[:, 1] * second[:, 0], axis=0))
    return jnp.stack([real_part, imag_part])

def adjoint_terms(spectra_shape, first_rows, second_rows, adjoint_split, stations):
    first = first_rows.astype(jnp.float32)
    second = second_rows.astype(jnp.float32)
    grad_real = adjoint_split[0].astype(jnp.float32)[None]
    grad_imag = adjoint_split[1].astype(jnp.float32)[None]
    to_first = jnp.stack([grad_real * second[:, 0] + grad_imag * second[:, 1], grad_real * second[:, 1] - grad_imag * second[:, 0]], axis=1)
    to_second = jnp.stack([grad_real * first[:, 0] - grad_imag * first[:, 1], grad_real * first[:, 1] + grad_imag * first[:, 0]], axis=1)
    result = jnp.zeros(spectra_shape, jnp.float32)
    result = result.at[:, :, :, stations[:, 0]].add(to_first.swapaxes(2, 3))
    result = result.at[:, :, :, stations[:, 1]].add(to_second.swapaxes(2, 3))
    return result

def reference(spectra, band_weights, pair_stations, block_live, windows, observed):

    def add_day(day, stack):
        rows = lax.dynamic_index_in_dim(spectra, day, 0, keepdims=True)
        first_rows, second_rows = station_rows(rows, pair_stations)
        return stack + cross_terms(first_rows, second_rows)
    stack = lax.fori_loop(0, DAYS, add_day, jnp.zeros((2, PAIRS, NF), jnp.float32))
    table = table_block(0, L, L)
    weights_full = jnp.concatenate([band_weights, band_weights], axis=1)
    pair_index = jnp.arange(PAIRS, dtype=jnp.int32)
    live_all = pair_index % PD < block_live[pair_index // PD]
    block = math.gcd(PAIRS, 64)
    forward_scale = 2.0 / math.sqrt(L * DAYS)
    adjoint_scale = 1.0 / math.sqrt(L)

    def one_block(index):
        first_pair = index * block
        piece = lax.dynamic_slice_in_dim(stack, first_pair, block, 1)
        flat_stack = jnp.concatenate([piece[0], piece[1]], axis=1)
        weighted = (flat_stack[:, None, :] * weights_full[None]).astype(jnp.bfloat16).reshape(block * BANDS, L)
        corr = forward_scale * jnp.dot(weighted, table, preferred_element_type=jnp.float32)
        window_rows = lax.dynamic_slice_in_dim(windows, first_pair, block, 0)
        lower_lag = window_rows[:, :, 0].reshape(-1)
        upper_lag = window_rows[:, :, 1].reshape(-1)
        row_live = jnp.repeat(lax.dynamic_slice_in_dim(live_all, first_pair, block, 0), BANDS)
        target = lax.dynamic_slice_in_dim(observed, first_pair, block, 0).reshape(block * BANDS, L).astype(jnp.float32)
        lag_index = jnp.arange(L, dtype=jnp.int32)
        inside = row_live[:, None] & (lag_index[None, :] >= lower_lag[:, None]) & (lag_index[None, :] < upper_lag[:, None])
        misfit = jnp.where(inside, corr - target, 0.0).astype(jnp.bfloat16)
        back = jnp.dot(misfit, table.T, preferred_element_type=jnp.float32)
        summed = lax.optimization_barrier(jnp.sum(back.reshape(block, BANDS, L) * weights_full[None], axis=1))
        return adjoint_scale * summed
    adjoint_spec = lax.map(one_block, jnp.arange(PAIRS // block, dtype=jnp.int32)).reshape(PAIRS, L)
    adjoint_split = adjoint_spec.reshape(PAIRS, 2, NF).transpose(1, 0, 2)

    def one_day(day):
        rows = lax.dynamic_index_in_dim(spectra, day, 0, keepdims=True)
        first_rows, second_rows = station_rows(rows, pair_stations)
        return adjoint_terms(rows.shape, first_rows, second_rows, adjoint_split, pair_stations)[0]
    return lax.map(one_day, jnp.arange(DAYS, dtype=jnp.int32))
```

```python
import functools
import math

import jax
import jax.numpy as jnp
import numpy as np
from jax import lax
from jax.experimental import pallas as pl
from jax.experimental.pallas import tpu as pltpu
from jax.sharding import PartitionSpec as P

F32 = jnp.float32
BF16 = jnp.bfloat16
MESH = pl.DeviceIdType.MESH
FINE = 32


def split_const(table):
    high = table.astype(jnp.bfloat16)
    low = (table - high.astype(np.float64)).astype(jnp.bfloat16)
    return high, low


@functools.lru_cache(maxsize=None)
def tables(y_lo, n_z):
    count = y_lo * n_z
    coarse = 2 * count
    width = 2 * coarse
    lags = FINE * width
    lanes = 4 * count
    cos_c = np.zeros((4 * lanes, 6 * width))
    t_a = np.arange(width)
    for c in range(2):
        for h in range(2):
            for z in range(n_z):
                for y in range(y_lo):
                    index = 2 * (y * n_z + z) + h
                    angle = 2 * np.pi * ((index * t_a) % width) / width
                    real, imag = (np.cos(angle), np.sin(angle)) if c == 0 else (-np.sin(angle), np.cos(angle))
                    for q in range(3):
                        row = (c * 2 + h) * lanes + (z * 4 + q) * y_lo + y
                        cos_c[row, (2 * q) * width : (2 * q + 1) * width] = real
                        cos_c[row, (2 * q + 1) * width : (2 * q + 2) * width] = imag
    outer_high, outer_low = split_const(cos_c)
    back_high, back_low = split_const(np.ascontiguousarray(cos_c.T))
    fine = np.arange(FINE)
    angle = 2 * np.pi * ((fine[:, None] * fine[None, :]) % FINE) / FINE
    inner = np.concatenate([np.cos(angle), -np.sin(angle)], axis=1)
    inner_tables = np.concatenate(split_const(inner), axis=0)
    inner_back = np.concatenate(split_const(np.ascontiguousarray(inner.T)), axis=0)
    turn = 2 * np.pi * (fine[:, None] * t_a[None, :]) / lags
    twiddle = np.stack([np.cos(turn), np.sin(turn)]).astype(np.float32)
    return outer_high, outer_low, back_high, back_low, inner_tables, inner_back, twiddle


def kernel(dims, days, spec, ids, weights, live, windows, observed, outer_high_hbm, outer_low_hbm, back_high_hbm,
           back_low_hbm, inner, inner_back, twiddle, out, grads, turned, hot, rows, part, sib_in, xs, relay, x_in, y_out,
           y_in, z_out, z_in, z_out2, z_in2, y_out2, obs3, outer_high, outer_low, back_high, back_low, send_sem,
           recv_sem, table_sem):
    y_lo, n_z = dims
    n_y = 2 * y_lo
    chunk = n_y * 24
    half = chunk // 2
    width = 4 * y_lo * n_z
    lanes = width
    lags = FINE * width
    stations = spec.shape[3]
    pair = lax.axis_index("pair")
    day = lax.axis_index("day")
    z = lax.rem(pair, n_z)
    yl = pair // n_z
    yh = day // 8
    x = lax.rem(day // 2, 4)
    core = lax.rem(day, 2)
    y = yh * y_lo + yl

    sibling = {"day": day + 1 - 2 * core}
    right = {"day": yh * 8 + lax.rem(x + 1, 4) * 2 + core}
    left = {"day": yh * 8 + lax.rem(x + 3, 4) * 2 + core}

    def y_device(other):
        return {"pair": lax.rem(other, y_lo) * n_z + z, "day": (other // y_lo) * 8 + x * 2 + core}

    def z_device(other):
        return {"pair": yl * n_z + other}

    barrier = pltpu.get_barrier_semaphore()
    for device in (
        [sibling, right, left]
        + [y_device(lax.rem(y + step, n_y)) for step in range(1, n_y)]
        + [z_device(lax.rem(z + step, n_z)) for step in range(1, n_z)]
    ):
        pl.semaphore_signal(barrier, inc=1, device_id=device, device_id_type=MESH)

    table_copies = []
    for index, (source, target) in enumerate(
        [(outer_high_hbm, outer_high), (outer_low_hbm, outer_low), (back_high_hbm, back_high), (back_low_hbm, back_low)]
    ):
        copy = pltpu.make_async_copy(source, target, table_sem.at[index])
        copy.start()
        table_copies.append(copy)

    sent = []

    def send(source, target, index, device):
        copy = pltpu.make_async_remote_copy(
            src_ref=source,
            dst_ref=target,
            send_sem=send_sem.at[index],
            recv_sem=recv_sem.at[index],
            device_id=device,
            device_id_type=MESH,
        )
        copy.start()
        sent.append(copy)
        return copy

    flat = jnp.concatenate([spec[0, 0], spec[1, 0], spec[0, 1], spec[1, 1]], axis=0)
    turned[...] = flat.astype(F32).T.astype(BF16)
    station_index = lax.broadcasted_iota(jnp.int32, (chunk, stations), 1)
    low_lanes = lax.broadcasted_iota(jnp.int32, (chunk, 128), 1) < 64

    def cross(which, order):
        owner = lax.rem(x + order, 4)
        row = which * 4 + owner
        found = []
        for side in range(2):
            mark = (station_index == ids[row, :, side : side + 1]).astype(F32).astype(BF16)
            hot[side, row] = mark
            value = jnp.dot(mark, turned[...], preferred_element_type=F32)
            rows[side, row] = value.astype(BF16)
            found.append(value)
        first, second = found
        a_re, a_im = first[:, :128], first[:, 128:]
        b_re, b_im = second[:, :128], second[:, 128:]
        real = a_re * b_re + a_im * b_im
        imag = a_re * b_im - a_im * b_re
        real = real + pltpu.roll(real, 64, 1)
        imag = imag + pltpu.roll(imag, 64, 1)
        return jnp.where(low_lanes, real, imag)

    orders = (2, 1, 3, 0)
    sib = []
    first_half, second_half = pl.ds(0, half), pl.ds(half, half)

    def step_cross(step):
        def one(which, carry):
            part[which, step] = cross(jnp.where(which == 0, 1 - core, core), orders[step])
            return carry
        return one

    def summed(step):
        sib[step].wait_recv()
        return part[1, step] + sib_in[step]

    for step in range(4):
        lax.fori_loop(0, 2, step_cross(step), 0)
        if step == 0:
            pl.semaphore_wait(barrier, 3 + (n_y - 1) + (n_z - 1))
        sib.append(send(part.at[0, step], sib_in.at[step], step, sibling))
        if step == 1:
            xs[0] = summed(0)
            relay_right = send(xs.at[0, first_half], relay.at[0], 4, right)
            relay_left = send(xs.at[0, second_half], relay.at[1], 5, left)
        if step == 2:
            xs[1] = summed(1)
            arrive = [send(xs.at[1, second_half], x_in.at[0, second_half], 6, right)]
        if step == 3:
            xs[2] = summed(2)
            arrive.append(send(xs.at[2, first_half], x_in.at[1, first_half], 7, left))
    relay_right.wait_recv()
    xs[1, first_half] = xs[1, first_half] + relay[0]
    arrive.append(send(xs.at[1, first_half], x_in.at[0, first_half], 8, right))
    relay_left.wait_recv()
    xs[2, second_half] = xs[2, second_half] + relay[1]
    arrive.append(send(xs.at[2, second_half], x_in.at[1, second_half], 9, left))
    own = summed(3)

    for q in range(3):
        for t_b in range(FINE):
            obs3[8 * q : 8 * q + 8, t_b, :] = observed[q, :, t_b * width : (t_b + 1) * width].astype(F32)
    z_out[...] = jnp.zeros_like(z_out)

    for copy in arrive:
        copy.wait_recv()
    y_out[...] = (own + x_in[0] + x_in[1]).reshape(n_y, 24, 128)
    far_first = sorted(range(1, n_y), key=lambda step: -min(step, n_y - step))
    base = 10
    copies = []
    for step in far_first:
        other = lax.rem(y + step, n_y)
        copies.append(send(y_out.at[other], y_in.at[y], base + step - 1, y_device(other)))
    y_in[y] = y_out[y]
    base += n_y - 1
    for copy in copies:
        copy.wait_recv()
    for low in range(y_lo):
        total = y_in[low] + y_in[y_lo + low]
        for q in range(3):
            z_out[:, q * y_lo + low, :] = total[8 * q : 8 * q + n_z]
    z_far_first = sorted(range(1, n_z), key=lambda step: -min(step, n_z - step))
    copies = []
    for step in z_far_first:
        other = lax.rem(z + step, n_z)
        copies.append(send(z_out.at[other], z_in.at[z], base + step - 1, z_device(other)))
    z_in[z] = z_out[z]
    base += n_z - 1
    for copy in table_copies:
        copy.wait()
    for copy in copies:
        copy.wait_recv()

    stacked = z_in[...].reshape(lanes, 128).T
    blocks = []
    for c in range(2):
        for h in range(2):
            piece = stacked[(2 * c + h) * FINE : (2 * c + h + 1) * FINE]
            scaled = weights[:, h * FINE : (h + 1) * FINE, :] * piece[None]
            blocks.append(scaled.reshape(8 * FINE, lanes).astype(BF16))
    left_side = jnp.concatenate(blocks, axis=1)
    outer = jnp.dot(left_side, outer_high[...], preferred_element_type=F32) + jnp.dot(
        left_side, outer_low[...], preferred_element_type=F32
    )
    cosine, sine = twiddle[0], twiddle[1]
    columns = []
    for q in range(3):
        real = outer[:, 2 * q * width : (2 * q + 1) * width].reshape(8, FINE, width)
        imag = outer[:, (2 * q + 1) * width : (2 * q + 2) * width].reshape(8, FINE, width)
        new_real = real * cosine[None] - imag * sine[None]
        new_imag = real * sine[None] + imag * cosine[None]
        for k in range(8):
            columns.append(jnp.concatenate([new_real[k], new_imag[k]], axis=0))
    middle = jnp.concatenate(columns, axis=1)
    high = middle.astype(BF16)
    low_part = (middle - high.astype(F32)).astype(BF16)
    product = jnp.dot(inner[...], high, preferred_element_type=F32)
    corr = product[:FINE] + product[FINE:] + jnp.dot(inner[:FINE], low_part, preferred_element_type=F32)
    forward_scale = 2.0 / math.sqrt(lags * days)
    lag_index = lax.broadcasted_iota(jnp.int32, (FINE, width), 0) * width + lax.broadcasted_iota(
        jnp.int32, (FINE, width), 1
    )
    alive = live[0]
    pieces = []
    for q in range(3):
        for k in range(8):
            r = 8 * q + k
            upper = jnp.where(q < alive, windows[q, k, 1], 0)
            inside = (lag_index >= windows[q, k, 0]) & (lag_index < upper)
            gap = forward_scale * corr[:, r * width : (r + 1) * width] - obs3[r]
            pieces.append(jnp.where(inside, gap, 0.0).astype(BF16))
    misfit = jnp.concatenate(pieces, axis=1)
    product = jnp.dot(inner_back[...], misfit, preferred_element_type=F32)
    spread = product[: 2 * FINE] + product[2 * FINE :]
    lines = []
    for k in range(8):
        line = []
        for q in range(3):
            r = 8 * q + k
            real = spread[:FINE, r * width : (r + 1) * width]
            imag = spread[FINE:, r * width : (r + 1) * width]
            line.append(real * cosine + imag * sine)
            line.append(imag * cosine - real * sine)
        lines.append(jnp.concatenate(line, axis=1))
    left_side = jnp.concatenate(lines, axis=0)
    high = left_side.astype(BF16)
    low_part = (left_side - high.astype(F32)).astype(BF16)
    bands = (
        jnp.dot(high, back_high[...], preferred_element_type=F32)
        + jnp.dot(high, back_low[...], preferred_element_type=F32)
        + jnp.dot(low_part, back_high[...], preferred_element_type=F32)
    )
    adjoint_scale = 1.0 / math.sqrt(lags)
    blocks = []
    for c in range(2):
        for h in range(2):
            piece = bands[:, (2 * c + h) * lanes : (2 * c + h + 1) * lanes].reshape(8, FINE, lanes)
            blocks.append(adjoint_scale * jnp.sum(piece * weights[:, h * FINE : (h + 1) * FINE, :], axis=0))
    z_out2[...] = jnp.concatenate(blocks, axis=0).T.reshape(n_z, 4 * y_lo, 128)

    copies = []
    for step in z_far_first:
        other = lax.rem(z + step, n_z)
        copies.append(send(z_out2.at[other], z_in2.at[z], base + step - 1, z_device(other)))
    z_in2[z] = z_out2[z]
    base += n_z - 1
    for copy in copies:
        copy.wait_recv()
    if n_z < 8:
        y_out2[...] = jnp.zeros_like(y_out2)
    for low in range(y_lo):
        for q in range(3):
            y_out2[low, 8 * q : 8 * q + n_z, :] = z_in2[:, q * y_lo + low, :]
    here = core * 4 + x
    copies = []
    for step in far_first:
        other = lax.rem(y + step, n_y)
        copies.append(
            send(y_out2.at[lax.rem(other, y_lo)], grads.at[here, pl.ds(pl.multiple_of(y * 24, 8), 24)], base + step - 1,
                 y_device(other))
        )
    grads[here, pl.ds(pl.multiple_of(y * 24, 8), 24)] = y_out2[yl]
    base += n_y - 1
    for copy in copies:
        copy.wait_recv()

    from_left = core * 4 + lax.rem(x + 3, 4)
    from_right = core * 4 + lax.rem(x + 1, 4)
    across = core * 4 + lax.rem(x + 2, 4)
    go_right = send(grads.at[here], grads.at[here], base, right)
    go_left = send(grads.at[here], grads.at[here], base + 1, left)
    ends = [send(grads.at[here], grads.at[here], base + 4, sibling)]
    go_right.wait_recv()
    pass_right = send(grads.at[from_left, first_half], grads.at[from_left, first_half], base + 2, right)
    go_left.wait_recv()
    pass_left = send(grads.at[from_right, second_half], grads.at[from_right, second_half], base + 3, left)
    ends.append(send(grads.at[from_left], grads.at[from_left], base + 5, sibling))
    ends.append(send(grads.at[from_right], grads.at[from_right], base + 6, sibling))
    pass_right.wait_recv()
    pass_left.wait_recv()
    ends.append(send(grads.at[across], grads.at[across], base + 7, sibling))

    def add(which, order):
        owner = lax.rem(x + order, 4)
        row = which * 4 + owner
        grad = grads[row]
        other = pltpu.roll(grad, 64, 1)
        g_re = jnp.where(low_lanes, grad, other)
        g_im = jnp.where(low_lanes, other, grad)
        first = rows[0, row].astype(F32)
        second = rows[1, row].astype(F32)
        a_re, a_im = first[:, :128], first[:, 128:]
        b_re, b_im = second[:, :128], second[:, 128:]
        to_first = jnp.concatenate([g_re * b_re + g_im * b_im, g_re * b_im - g_im * b_re], axis=1)
        to_second = jnp.concatenate([g_re * a_re - g_im * a_im, g_re * a_im + g_im * a_re], axis=1)
        dims_t = (((1,), (0,)), ((), ()))
        total = lax.dot_general(to_first.T.astype(BF16), hot[0, row], dims_t, preferred_element_type=F32)
        return total + lax.dot_general(to_second.T.astype(BF16), hot[1, row], dims_t, preferred_element_type=F32)

    def put(value, fresh):
        for c in range(2):
            for d in range(2):
                piece = value[c * 128 + d * 64 : c * 128 + d * 64 + 64]
                out[d, c] = piece if fresh else out[d, c] + piece

    put(add(core, 0), True)
    for order in (3, 1, 2):
        put(add(core, order), False)
    for copy in ends:
        copy.wait_recv()

    def add_step(order, carry):
        put(add(1 - core, order), False)
        return carry

    lax.fori_loop(0, 4, add_step, 0)
    for copy in sent:
        copy.wait_send()


def body(y_lo, n_z, spectra, band_weights, pair_stations, block_live, windows, observed):
    n_y = 2 * y_lo
    chunk = n_y * 24
    lanes = 4 * y_lo * n_z
    width = lanes
    stations = spectra.shape[3]
    ids = (
        pair_stations.reshape(y_lo, n_z, 2, 4, 2, 3, 2).transpose(4, 3, 2, 0, 5, 1, 6).reshape(8, n_y, 3, n_z, 2)
    )
    if n_z < 8:
        ids = jnp.pad(ids, ((0, 0), (0, 0), (0, 0), (0, 8 - n_z), (0, 0)), constant_values=-1)
    ids = ids.reshape(8, chunk, 2)
    weights = band_weights.reshape(8, y_lo, n_z, 2, FINE).transpose(0, 3, 4, 2, 1)
    weights = jnp.broadcast_to(weights[:, :, :, :, None, :], (8, 2, FINE, n_z, 4, y_lo)).reshape(8, 2 * FINE, lanes)
    outer_high, outer_low, back_high, back_low, inner, inner_back, twiddle = tables(y_lo, n_z)
    n_sem = 10 + 2 * (n_y - 1) + 2 * (n_z - 1) + 8
    vmem = pl.BlockSpec(memory_space=pltpu.VMEM)
    smem = pl.BlockSpec(memory_space=pltpu.SMEM)
    anywhere = pl.BlockSpec(memory_space=pl.ANY)
    return pl.pallas_call(
        functools.partial(kernel, (y_lo, n_z), 32),
        out_shape=jax.ShapeDtypeStruct(spectra.shape, F32),
        in_specs=[vmem, vmem, vmem, smem, smem, vmem, anywhere, anywhere, anywhere, anywhere, vmem, vmem, vmem],
        out_specs=vmem,
        scratch_shapes=[
            pltpu.VMEM((8, chunk, 128), F32),
            pltpu.VMEM((stations, 256), BF16),
            pltpu.VMEM((2, 8, chunk, stations), BF16),
            pltpu.VMEM((2, 8, chunk, 256), BF16),
            pltpu.VMEM((2, 4, chunk, 128), F32),
            pltpu.VMEM((4, chunk, 128), F32),
            pltpu.VMEM((3, chunk, 128), F32),
            pltpu.VMEM((2, chunk // 2, 128), F32),
            pltpu.VMEM((2, chunk, 128), F32),
            pltpu.VMEM((n_y, 24, 128), F32),
            pltpu.VMEM((n_y, 24, 128), F32),
            pltpu.VMEM((n_z, 4 * y_lo, 128), F32),
            pltpu.VMEM((n_z, 4 * y_lo, 128), F32),
            pltpu.VMEM((n_z, 4 * y_lo, 128), F32),
            pltpu.VMEM((n_z, 4 * y_lo, 128), F32),
            pltpu.VMEM((y_lo, 24, 128), F32),
            pltpu.VMEM((24, FINE, width), F32),
            pltpu.VMEM(outer_high.shape, BF16),
            pltpu.VMEM(outer_low.shape, BF16),
            pltpu.VMEM(back_high.shape, BF16),
            pltpu.VMEM(back_low.shape, BF16),
            pltpu.SemaphoreType.DMA((n_sem,)),
            pltpu.SemaphoreType.DMA((n_sem,)),
            pltpu.SemaphoreType.DMA((4,)),
        ],
        compiler_params=pltpu.CompilerParams(
            collective_id=0, has_side_effects=True, vmem_limit_bytes=50 * 1024 * 1024
        ),
    )(
        spectra, ids, weights, block_live, windows, observed,
        jnp.asarray(outer_high), jnp.asarray(outer_low), jnp.asarray(back_high), jnp.asarray(back_low),
        jnp.asarray(inner), jnp.asarray(inner_back), jnp.asarray(twiddle),
    )


def solution(mesh, y_lo=None):
    n_pair = mesh.shape["pair"]
    y_lo = y_lo or max(1, n_pair // 8)
    in_specs = (
        P("day", None, "pair", None),
        P(),
        P(),
        P(("pair", "day")),
        P(("pair", "day"), None, None),
        P(("pair", "day"), None, None),
    )
    out_specs = P("day", None, "pair", None)
    return jax.shard_map(
        functools.partial(body, y_lo, n_pair // y_lo), mesh=mesh, in_specs=in_specs, out_specs=out_specs, check_vma=False
    )
```
